32 devices in a mesh: dp: 2 (over core), seq: 16 (over z, y, x).
Axes of the slice: x: 2, y: 2, z: 4, core: 2. Of those that a mesh axis runs over, the one named last changes fastest.
Arguments:
- queries: bfloat16 [16384, 768], P(('dp', 'seq')), parts along dimension 0, may hold values from -11 to 11
- key_states: bfloat16 [16384, 768], P(('dp', 'seq')), parts along dimension 0, may hold values from -11 to 11
- value_states: bfloat16 [16384, 768], P(('dp', 'seq')), parts along dimension 0, may hold values from -6 to 6
- out_weight: bfloat16 [768, 1536], P('seq'), may hold values from -0.21875 to 0.21875
- block_picks: int32 [32, 6, 2], P(('dp', 'seq')), parts along dimension 0, may hold values from 0 to 3, as said below
- slot_counts: int32 [32, 6], P(('dp', 'seq')), parts along dimension 0, may hold values from 1 to 2, as said below
Outputs:
- projected: bfloat16 [16384, 1536], P(('dp', 'seq')), parts along dimension 0
The draws below stay inside these ranges and needn't reach their ends.
There are 2 independent parts, one for each index of `dp`. The reference program is written for one: setup_inputs(seed, part) draws one part's arguments, and reference() takes and returns one part's arrays. A program takes and returns all parts, laid end to end along the dimension named above; an argument that names none is the same for every part. Nothing has to cross between parts.
Inputs may be any that keep to these rules, and one draw needn't show every extreme that they name: Each block_picks[s, j] holds 2 different spatial blocks of shard s. `slot_counts`: in every draw some shard has 2 in every direction.
All inputs are finite; a program needn't handle non-finite values.
Results may differ from the reference program's by a relative error of at most 0.0057.
Values may be sent and summed in bfloat16 or wider, within the bound.
A program may use at most 64 MiB of HBM per device.

```python
import jax
import jax.numpy as jnp
from jax import lax

D = 1536
HEADS = 6
HD = 128
BLOCK = 128
NB = 4
LEVELS = 3
CAP = 2
DIRS = 6
TOK_DEV = 512
TOKENS = 8192
N_SEQ = 16


def draw_queries(key, part):
    key = jax.random.fold_in(key, 1)
    return jax.random.normal(key, (TOKENS, HEADS * HD), jnp.float32).astype(jnp.bfloat16)


def draw_key_states(key, part):
    key = jax.random.fold_in(key, 2)
    return jax.random.normal(key, (TOKENS, HEADS * HD), jnp.float32).astype(jnp.bfloat16)


def draw_block_picks(key, part):
    key = jax.random.fold_in(key, 3)
    scores = jax.random.randint(key, (N_SEQ, DIRS, NB), 0, 2 ** 20) * NB + jnp.arange(NB, dtype=jnp.int32)
    return jnp.argsort(scores, axis=-1)[..., :CAP].astype(jnp.int32)


def draw_slot_counts(key, part):
    key = jax.random.fold_in(key, 4)
    first_key, second_key, third_key = jax.random.split(key, 3)
    spread = 2 ** (jnp.arange(DIRS, dtype=jnp.int32) % LEVELS)
    coin = jax.random.randint(first_key, (N_SEQ, DIRS), 0, 2 ** 16) % spread[None, :]
    lower = jax.random.randint(second_key, (N_SEQ, DIRS), 1, CAP + 1)
    counted = jnp.where(coin == 0, CAP, lower)
    full_row = jax.random.randint(third_key, (), 0, N_SEQ)
    counted = jnp.where((jnp.arange(N_SEQ) == full_row)[:, None], CAP, counted)
    return counted.astype(jnp.int32)


def shard_levels(key, shape, pieces, smallest, top_value):
    def one(position, blocks):
        steps = jax.random.uniform(jax.random.fold_in(jax.random.fold_in(key, 6), position), (blocks,), jnp.float32, smallest / len(pieces), top_value / len(pieces))
        return jnp.repeat(jnp.exp(steps), shape[position] // blocks).reshape((-1,) + (1,) * (len(shape) - position - 1))

    loudness = one(*pieces[0])
    for cut in pieces[1:]:
        loudness = loudness * one(*cut)
    return loudness


def noise(own_key, shape, scale, most, cuts=(), kind=jnp.bfloat16):
    array = jax.random.normal(own_key, shape, jnp.float32) * scale
    if len(cuts) > 0:
        array = shard_levels(own_key, shape, cuts, -0.22, 0.18) * array
    return jnp.clip(array, min=-most, max=most).astype(kind)


def setup_inputs(seed: int = 0, part: int = 0) -> dict:
    key_of = jax.random.split(jax.random.key(seed), 7)
    part_splits = jax.random.split(jax.random.fold_in(key_of[6], part), 7)
    return {
        "queries": draw_queries(jax.random.fold_in(jax.random.fold_in(key_of[6], part), 71), part),
        "key_states": draw_key_states(jax.random.fold_in(jax.random.fold_in(key_of[6], part), 71), part),
        "value_states": noise(part_splits[2], (TOKENS, HEADS * HD), 1.0, 6.0, ((0, 16),)),
        "out_weight": noise(key_of[3], (HEADS * HD, D), (HEADS * HD) ** -0.5, 0.21875, ((0, 16),)),
        "block_picks": draw_block_picks(jax.random.fold_in(jax.random.fold_in(key_of[6], part), 71), part),
        "slot_counts": draw_slot_counts(jax.random.fold_in(jax.random.fold_in(key_of[6], part), 71), part),
    }


def attend_rows(query_rows, key_rows, value_rows, key_live):
    outputs = []
    for head_index in range(HEADS):
        head_cols = slice(head_index * HD, (head_index + 1) * HD)
        scores = jnp.dot(query_rows[:, head_cols], key_rows[:, head_cols].T, preferred_element_type=jnp.float32) * (HD ** -0.5)
        scores = jnp.where(key_live[None, :], scores, -jnp.inf)
        row_max = jnp.max(scores, axis=1, keepdims=True)
        weights = jnp.exp(scores - row_max)
        denominator = jnp.sum(weights, axis=1, keepdims=True)
        weighted = jnp.dot(weights.astype(jnp.bfloat16), value_rows[:, head_cols], preferred_element_type=jnp.float32)
        outputs.append(weighted / denominator)
    return jnp.concatenate(outputs, axis=1).astype(jnp.bfloat16)


def shard_output(queries, key_states, value_states, out_weight, block_picks, slot_counts, shard_index):
    first_tok = (shard_index * TOK_DEV).astype(jnp.int32)
    query_rows = lax.dynamic_slice_in_dim(queries, first_tok, TOK_DEV, 0)
    key_list = [lax.dynamic_slice_in_dim(key_states, first_tok, TOK_DEV, 0)]
    value_list = [lax.dynamic_slice_in_dim(value_states, first_tok, TOK_DEV, 0)]
    live_list = [jnp.ones((TOK_DEV,), bool)]
    for direction in range(DIRS):
        distance = 2 ** (direction % LEVELS)
        sender = shard_index - distance if direction < LEVELS else shard_index + distance
        in_range = (sender >= 0) & (sender < N_SEQ)
        clipped = jnp.clip(sender, 0, N_SEQ - 1).astype(jnp.int32)
        chosen = block_picks[clipped, direction]
        live_count = slot_counts[clipped, direction]
        for slot_index in range(CAP):
            first_row = (clipped * TOK_DEV + chosen[slot_index] * BLOCK).astype(jnp.int32)
            key_list.append(lax.dynamic_slice_in_dim(key_states, first_row, BLOCK, 0))
            value_list.append(lax.dynamic_slice_in_dim(value_states, first_row, BLOCK, 0))
            live_list.append(jnp.broadcast_to(in_range & (slot_index < live_count), (BLOCK,)))
    attended = attend_rows(query_rows, jnp.concatenate(key_list, 0), jnp.concatenate(value_list, 0), jnp.concatenate(live_list, 0))
    return jnp.dot(attended, out_weight, preferred_element_type=jnp.float32).astype(jnp.bfloat16)


def reference(queries, key_states, value_states, out_weight, block_picks, slot_counts):
    def one_shard(shard_index):
        return shard_output(queries, key_states, value_states, out_weight, block_picks, slot_counts, shard_index)

    shard_ids = jnp.arange(N_SEQ, dtype=jnp.int32)
    outputs = lax.map(one_shard, shard_ids)
    return outputs.reshape(N_SEQ * TOK_DEV, D)
```

```python
import functools

import jax
import jax.numpy as jnp
from jax import lax
from jax.experimental import pallas as pl
from jax.experimental.pallas import tpu as pltpu
from jax.sharding import PartitionSpec as P

HD = 128
BLOCK = 128
LEVELS = 3
DIRS = 2 * LEVELS
MASKED = -1e30
SEND_ORDER = (1, 4, 0, 3, 2, 5)
WORK_ORDER = (2, 5, 0, 3, 1, 4)


def hop(direction):
    size = 2 ** (direction % LEVELS)
    return size if direction < LEVELS else -size


def kernel(
    n, q_ref, k_ref, v_ref, w_ref, picks_ref, counts_ref, out_ref, wout_ref,
    pack, mark, got, got_mark, acc, top, total,
    pack_send, pack_recv, mark_send, mark_recv, w_send, w_recv, own_sem, pair_send, pair_recv,
):
    me = lax.axis_index("seq")
    dp = lax.axis_index("dp")
    sibling = dp + 1 - 2 * (dp % 2)
    rows, width = q_ref.shape
    heads = width // HD
    slots = picks_ref.shape[1]
    bits = n.bit_length() - 1
    half_cols = w_ref.shape[1] // 2
    half = pl.ds(pl.multiple_of((dp % 2) * half_cols, half_cols), half_cols)

    def partner(bit):
        return me + 2**bit * (1 - 2 * ((me // 2**bit) % 2))

    def inside(shard):
        return jnp.logical_and(shard >= 0, shard < n)

    barrier = pltpu.get_barrier_semaphore()
    expected = jnp.int32(bits + 1)
    for direction in range(DIRS):
        other = me + hop(direction)
        expected = expected + inside(other).astype(jnp.int32)

        @pl.when(inside(other))
        def _(other=other):
            pl.semaphore_signal(
                barrier, inc=1, device_id=(dp, other), device_id_type=pl.DeviceIdType.MESH
            )
    for bit in range(bits):
        pl.semaphore_signal(
            barrier, inc=1, device_id=(dp, partner(bit)), device_id_type=pl.DeviceIdType.MESH
        )
    pl.semaphore_signal(
        barrier, inc=1, device_id=(sibling, me), device_id_type=pl.DeviceIdType.MESH
    )

    own = pltpu.make_async_copy(w_ref.at[:, half], wout_ref.at[me, :, half], own_sem)
    own.start()

    def fill(direction):
        for slot in range(slots):
            block = picks_ref[direction, slot]
            at = pl.ds(slot * BLOCK, BLOCK)
            pack[direction, 0, at, :] = k_ref[block]
            pack[direction, 1, at, :] = v_ref[block]
            live = counts_ref[0, direction] > slot
            mark[direction, slot] = jnp.full((8, HD), jnp.where(live, 0.0, MASKED), jnp.float32)

    def pack_copies(direction):
        to = (dp, me + hop(direction))
        return (
            pltpu.make_async_remote_copy(
                pack.at[direction], got.at[direction],
                pack_send.at[direction], pack_recv.at[direction],
                device_id=to, device_id_type=pl.DeviceIdType.MESH,
            ),
            pltpu.make_async_remote_copy(
                mark.at[direction], got_mark.at[direction],
                mark_send.at[direction], mark_recv.at[direction],
                device_id=to, device_id_type=pl.DeviceIdType.MESH,
            ),
        )

    def weight_copies(step):
        bit = bits - 1 - step
        span = 2 ** (bit + 1)
        copies = []
        for i in range(2**step):
            place = wout_ref.at[me % span + i * span, :, half]
            index = 2**step - 1 + i
            copies.append(
                pltpu.make_async_remote_copy(
                    place, place, w_send.at[index], w_recv.at[index],
                    device_id=(dp, partner(bit)), device_id_type=pl.DeviceIdType.MESH,
                )
            )
        return copies

    pair = pltpu.make_async_remote_copy(
        wout_ref.at[:, :, half], wout_ref.at[:, :, half], pair_send, pair_recv,
        device_id=(sibling, me), device_id_type=pl.DeviceIdType.MESH,
    )

    def weight_step(step):
        if step > bits:
            return
        if step > 0:
            for copy in weight_copies(step - 1):
                copy.wait_recv()
        if step < bits:
            for copy in weight_copies(step):
                copy.start()
        else:
            pair.start()

    fill(SEND_ORDER[0])
    pl.semaphore_wait(barrier, expected)
    for place, direction in enumerate(SEND_ORDER):
        if place > 0:
            fill(direction)

        @pl.when(inside(me + hop(direction)))
        def _(direction=direction):
            for copy in pack_copies(direction):
                copy.start()

        if place == 0:
            own.wait()
            weight_step(0)

    scale = HD**-0.5
    tiles = 2
    tile = rows // tiles

    def local_head(h, carry):
        cols = pl.ds(pl.multiple_of(h * HD, HD), HD)
        keys = k_ref[:, :, cols].reshape(rows, HD)
        values = v_ref[:, :, cols].reshape(rows, HD)
        for t in range(tiles):
            at = pl.ds(t * tile, tile)
            scores = lax.dot_general(
                q_ref[at, cols], keys, (((1,), (1,)), ((), ())),
                preferred_element_type=jnp.float32,
            ) * scale
            high = jnp.max(scores, axis=1, keepdims=True)
            weights = jnp.exp(scores - high)
            top[h, at, :] = high
            total[h, at, :] = jnp.sum(weights, axis=1, keepdims=True)
            acc[h, at, :] = jnp.dot(
                weights.astype(jnp.bfloat16), values, preferred_element_type=jnp.float32
            )
        return carry

    lax.fori_loop(0, heads, local_head, 0)
    weight_step(1)

    def far_head(direction, h):
        cols = pl.ds(pl.multiple_of(h * HD, HD), HD)
        keys = got[direction, 0, :, cols]
        values = got[direction, 1, :, cols]
        bias = jnp.concatenate(
            [got_mark[direction, slot, 0:1, :] for slot in range(slots)], axis=1
        )
        for t in range(tiles):
            at = pl.ds(t * tile, tile)
            scores = lax.dot_general(
                q_ref[at, cols], keys, (((1,), (1,)), ((), ())),
                preferred_element_type=jnp.float32,
            ) * scale + bias
            before = top[h, at, :]
            high = jnp.maximum(before, jnp.max(scores, axis=1, keepdims=True))
            shrink = jnp.exp(before - high)
            weights = jnp.exp(scores - high)
            top[h, at, :] = high
            total[h, at, :] = total[h, at, :] * shrink + jnp.sum(weights, axis=1, keepdims=True)
            acc[h, at, :] = acc[h, at, :] * shrink + jnp.dot(
                weights.astype(jnp.bfloat16), values, preferred_element_type=jnp.float32
            )

    for place, direction in enumerate(WORK_ORDER):

        @pl.when(inside(me - hop(direction)))
        def _(direction=direction):
            for copy in pack_copies(direction):
                copy.wait_recv()

            def body(h, carry):
                far_head(direction, h)
                return carry

            lax.fori_loop(0, heads, body, 0)

        weight_step(place + 2)
    for step in range(DIRS + 2, bits + 1):
        weight_step(step)

    for h in range(heads):
        out_ref[:, h * HD : (h + 1) * HD] = (acc[h] / total[h]).astype(out_ref.dtype)

    for direction in range(DIRS):

        @pl.when(inside(me + hop(direction)))
        def _(direction=direction):
            for copy in pack_copies(direction):
                copy.wait_send()

    for step in range(bits):
        for copy in weight_copies(step):
            copy.wait_send()
    pair.wait()


def shards(queries, key_states, value_states, out_weight, block_picks, slot_counts):
    n = lax.axis_size("seq")
    rows, width = queries.shape
    slots = block_picks.shape[2]
    heads = width // HD
    blocks = rows // BLOCK
    vmem = pl.BlockSpec(memory_space=pltpu.VMEM)
    smem = pl.BlockSpec(memory_space=pltpu.SMEM)
    dma = pltpu.SemaphoreType.DMA
    attended, weight = pl.pallas_call(
        functools.partial(kernel, n),
        out_shape=(
            jax.ShapeDtypeStruct((rows, width), jnp.bfloat16),
            jax.ShapeDtypeStruct((n,) + out_weight.shape, jnp.bfloat16),
        ),
        in_specs=[vmem, vmem, vmem, vmem, smem, smem],
        out_specs=(vmem, pl.BlockSpec(memory_space=pl.ANY)),
        scratch_shapes=[
            pltpu.VMEM((DIRS, 2, slots * BLOCK, width), jnp.bfloat16),
            pltpu.VMEM((DIRS, slots, 8, HD), jnp.float32),
            pltpu.VMEM((DIRS, 2, slots * BLOCK, width), jnp.bfloat16),
            pltpu.VMEM((DIRS, slots, 8, HD), jnp.float32),
            pltpu.VMEM((heads, rows, HD), jnp.float32),
            pltpu.VMEM((heads, rows, 1), jnp.float32),
            pltpu.VMEM((heads, rows, 1), jnp.float32),
            dma((DIRS,)), dma((DIRS,)), dma((DIRS,)), dma((DIRS,)),
            dma((n,)), dma((n,)), dma, dma, dma,
        ],
        compiler_params=pltpu.CompilerParams(
            collective_id=0, has_side_effects=True, vmem_limit_bytes=48 * 2**20
        ),
    )(
        queries,
        key_states.reshape(blocks, BLOCK, width),
        value_states.reshape(blocks, BLOCK, width),
        out_weight,
        block_picks[0],
        slot_counts,
    )
    result = jnp.dot(
        attended, weight.reshape(-1, weight.shape[2]), preferred_element_type=jnp.float32
    )
    return result.astype(jnp.bfloat16)


def solution(mesh):
    placed = (
        P(("dp", "seq"), None),
        P(("dp", "seq"), None),
        P(("dp", "seq"), None),
        P("seq", None),
        P(("dp", "seq"), None, None),
        P(("dp", "seq"), None),
    )
    return jax.shard_map(
        shards, mesh=mesh, in_specs=placed, out_specs=P(("dp", "seq"), None), check_vma=False
    )
```

```python
import functools

import jax
import jax.numpy as jnp
from jax import lax
from jax.experimental import pallas as pl
from jax.experimental.pallas import tpu as pltpu
from jax.sharding import PartitionSpec as P

HD = 128
BLOCK = 128
LEVELS = 3
DIRS = 2 * LEVELS
MASKED = -1e30
LEVEL_ORDER = (1, 2, 0)


def hop(direction):
    size = 2 ** (direction % LEVELS)
    return size if direction < LEVELS else -size


def kernel(
    n, q_ref, k_ref, v_ref, w_ref, picks_ref, counts_ref, out_ref, wout_ref,
    pack, mark, got, got_mark, acc, top, total,
    pack_send, pack_recv, mark_send, mark_recv, w_send, w_recv, own_sem,
):
    me = lax.axis_index("seq")
    dp = lax.axis_index("dp")
    sibling = dp + 1 - 2 * (dp % 2)
    rows, width = q_ref.shape
    heads = width // HD
    slots = picks_ref.shape[1]
    half_cols = w_ref.shape[1] // 2
    half = pl.ds(pl.multiple_of((dp % 2) * half_cols, half_cols), half_cols)

    near = me + 1 - 2 * (me % 2)
    others = n // 2

    def inside(shard):
        return jnp.logical_and(shard >= 0, shard < n)

    barrier = pltpu.get_barrier_semaphore()
    expected = jnp.int32(others + 1)
    for direction in range(DIRS):
        other = me + hop(direction)
        expected = expected + inside(other).astype(jnp.int32)

        @pl.when(inside(other))
        def _(other=other):
            pl.semaphore_signal(
                barrier, inc=1, device_id=(dp, other), device_id_type=pl.DeviceIdType.MESH
            )
    for other in [near] + [(me + 2 * j) % n for j in range(1, others)]:
        pl.semaphore_signal(
            barrier, inc=1, device_id=(dp, other), device_id_type=pl.DeviceIdType.MESH
        )
    pl.semaphore_signal(
        barrier, inc=1, device_id=(sibling, me), device_id_type=pl.DeviceIdType.MESH
    )

    own = pltpu.make_async_copy(w_ref.at[:, half], wout_ref.at[me, :, half], own_sem)
    own.start()

    def fill(direction, slot):
        block = picks_ref[direction, slot]
        pack[direction, slot, 0] = k_ref[block]
        pack[direction, slot, 1] = v_ref[block]

    def fill_mark(direction):
        for slot in range(slots):
            live = counts_ref[0, direction] > slot
            mark[direction, slot] = jnp.full((8, HD), jnp.where(live, 0.0, MASKED), jnp.float32)

    def pack_copy(direction, slot):
        return pltpu.make_async_remote_copy(
            pack.at[direction, slot],
            got.at[direction % LEVELS, slot, :, direction // LEVELS],
            pack_send.at[direction, slot], pack_recv.at[direction, slot],
            device_id=(dp, me + hop(direction)), device_id_type=pl.DeviceIdType.MESH,
        )

    def mark_copy(direction):
        return pltpu.make_async_remote_copy(
            mark.at[direction], got_mark.at[direction],
            mark_send.at[direction], mark_recv.at[direction],
            device_id=(dp, me + hop(direction)), device_id_type=pl.DeviceIdType.MESH,
        )

    def sibling_arrival(j, same):
        shard = ((me if same else near) + n - 2 * j) % n
        other_half = pl.ds(pl.multiple_of((1 - dp % 2) * half_cols, half_cols), half_cols)
        place = wout_ref.at[shard, :, other_half]
        index = n + j + (0 if same else others)
        return pltpu.make_async_remote_copy(
            place, place, w_send.at[index], w_recv.at[index],
            device_id=(sibling, me), device_id_type=pl.DeviceIdType.MESH,
        )

    def send(level, slot):
        for direction in (level, level + LEVELS):
            fill(direction, slot)
            if slot == 0:
                fill_mark(direction)

            @pl.when(inside(me + hop(direction)))
            def _(direction=direction):
                if slot == 0:
                    mark_copy(direction).start()
                pack_copy(direction, slot).start()

    def weight_copy(shard, index, to):
        place = wout_ref.at[shard, :, half]
        return pltpu.make_async_remote_copy(
            place, place, w_send.at[index], w_recv.at[index],
            device_id=to, device_id_type=pl.DeviceIdType.MESH,
        )

    def spread(j):
        return weight_copy(me, j, (dp, (me + 2 * j) % n))

    def spread_arrival(j):
        return weight_copy((me + n - 2 * j) % n, j, (dp, (me + 2 * j) % n))

    def across(j):
        return weight_copy((me + n - 2 * j) % n, others + j, (dp, near))

    def across_arrival(j):
        return weight_copy((near + n - 2 * j) % n, others + j, (dp, near))

    def pair(j, same):
        shard = ((me if same else near) + n - 2 * j) % n
        return weight_copy(shard, n + j + (0 if same else others), (sibling, me))

    for direction in range(DIRS):

        @pl.when(jnp.logical_not(inside(me - hop(direction))))
        def _(direction=direction):
            for slot in range(slots):
                for kind in range(2):
                    got[direction % LEVELS, slot, kind, direction // LEVELS] = jnp.zeros(
                        (BLOCK, width), jnp.bfloat16
                    )
            got_mark[direction] = jnp.full((slots, 8, HD), MASKED, jnp.float32)

    pl.semaphore_wait(barrier, expected)
    own.wait()
    for j in range(1, others):
        spread(j).start()
    across(0).start()
    pair(0, True).start()
    for level in LEVEL_ORDER[:2]:
        send(level, 0)

    scale = HD**-0.5
    tiles = 2
    tile = rows // tiles

    def local_head(h, carry):
        cols = pl.ds(pl.multiple_of(h * HD, HD), HD)
        keys = k_ref[:, :, cols].reshape(rows, HD)
        values = v_ref[:, :, cols].reshape(rows, HD)
        for t in range(tiles):
            at = pl.ds(t * tile, tile)
            scores = lax.dot_general(
                q_ref[at, cols], keys, (((1,), (1,)), ((), ())),
                preferred_element_type=jnp.float32,
            ) * scale
            high = jnp.max(scores, axis=1, keepdims=True)
            weights = jnp.exp(scores - high)
            top[h, at, :] = high
            total[h, at, :] = jnp.sum(weights, axis=1, keepdims=True)
            acc[h, at, :] = jnp.dot(
                weights.astype(jnp.bfloat16), values, preferred_element_type=jnp.float32
            )
        return carry

    lax.fori_loop(0, heads // 2, local_head, 0)
    for j in range(1, others):
        spread_arrival(j).wait_recv()
        across(j).start()
        pair(j, True).start()
    for level in LEVEL_ORDER[2:]:
        send(level, 0)
    lax.fori_loop(heads // 2, heads, local_head, 0)
    send(LEVEL_ORDER[0], 1)

    def far_head(level, slot, h):
        cols = pl.ds(pl.multiple_of(h * HD, HD), HD)
        keys = got[level, slot, 0, :, :, cols].reshape(2 * BLOCK, HD)
        values = got[level, slot, 1, :, :, cols].reshape(2 * BLOCK, HD)
        bias = jnp.concatenate(
            [got_mark[direction, slot, 0:1, :] for direction in (level, level + LEVELS)], axis=1
        )
        for t in range(tiles):
            at = pl.ds(t * tile, tile)
            scores = lax.dot_general(
                q_ref[at, cols], keys, (((1,), (1,)), ((), ())),
                preferred_element_type=jnp.float32,
            ) * scale + bias
            before = top[h, at, :]
            high = jnp.maximum(before, jnp.max(scores, axis=1, keepdims=True))
            shrink = jnp.exp(before - high)
            weights = jnp.exp(scores - high)
            top[h, at, :] = high
            total[h, at, :] = total[h, at, :] * shrink + jnp.sum(weights, axis=1, keepdims=True)
            acc[h, at, :] = acc[h, at, :] * shrink + jnp.dot(
                weights.astype(jnp.bfloat16), values, preferred_element_type=jnp.float32
            )

    def far(level, slot):
        for direction in (level, level + LEVELS):

            @pl.when(inside(me - hop(direction)))
            def _(direction=direction):
                if slot == 0:
                    mark_copy(direction).wait_recv()
                pack_copy(direction, slot).wait_recv()

        def body(h, carry):
            far_head(level, slot, h)
            return carry

        lax.fori_loop(0, heads, body, 0)

    far(LEVEL_ORDER[0], 0)
    for j in range(others):
        across_arrival(j).wait_recv()
        pair(j, False).start()
    for level in LEVEL_ORDER[1:]:
        send(level, 1)
    for level in LEVEL_ORDER[1:]:
        far(level, 0)
    for slot in range(1, slots):
        for level in LEVEL_ORDER:
            far(level, slot)

    for h in range(heads):
        out_ref[:, h * HD : (h + 1) * HD] = (acc[h] / total[h]).astype(out_ref.dtype)

    for direction in range(DIRS):

        @pl.when(inside(me + hop(direction)))
        def _(direction=direction):
            mark_copy(direction).wait_send()
            for slot in range(slots):
                pack_copy(direction, slot).wait_send()

    for j in range(others):
        if j > 0:
            spread(j).wait_send()
        across(j).wait_send()
    for same in (True, False):
        for j in range(others):
            pair(j, same).wait_send()
            sibling_arrival(j, same).wait_recv()


def shards(queries, key_states, value_states, out_weight, block_picks, slot_counts):
    n = lax.axis_size("seq")
    rows, width = queries.shape
    slots = block_picks.shape[2]
    heads = width // HD
    blocks = rows // BLOCK
    vmem = pl.BlockSpec(memory_space=pltpu.VMEM)
    smem = pl.BlockSpec(memory_space=pltpu.SMEM)
    dma = pltpu.SemaphoreType.DMA
    attended, weight = pl.pallas_call(
        functools.partial(kernel, n),
        out_shape=(
            jax.ShapeDtypeStruct((rows, width), jnp.bfloat16),
            jax.ShapeDtypeStruct((n,) + out_weight.shape, jnp.bfloat16),
        ),
        in_specs=[vmem, vmem, vmem, vmem, smem, smem],
        out_specs=(vmem, pl.BlockSpec(memory_space=pl.ANY)),
        scratch_shapes=[
            pltpu.VMEM((DIRS, slots, 2, BLOCK, width), jnp.bfloat16),
            pltpu.VMEM((DIRS, slots, 8, HD), jnp.float32),
            pltpu.VMEM((LEVELS, slots, 2, 2, BLOCK, width), jnp.bfloat16),
            pltpu.VMEM((DIRS, slots, 8, HD), jnp.float32),
            pltpu.VMEM((heads, rows, HD), jnp.float32),
            pltpu.VMEM((heads, rows, 1), jnp.float32),
            pltpu.VMEM((heads, rows, 1), jnp.float32),
            dma((DIRS, slots)), dma((DIRS, slots)), dma((DIRS,)), dma((DIRS,)),
            dma((2 * n,)), dma((2 * n,)), dma,
        ],
        compiler_params=pltpu.CompilerParams(
            collective_id=0, has_side_effects=True, vmem_limit_bytes=48 * 2**20
        ),
    )(
        queries,
        key_states.reshape(blocks, BLOCK, width),
        value_states.reshape(blocks, BLOCK, width),
        out_weight,
        block_picks[0],
        slot_counts,
    )
    result = jnp.dot(
        attended, weight.reshape(-1, weight.shape[2]), preferred_element_type=jnp.float32
    )
    return result.astype(jnp.bfloat16)


def solution(mesh):
    placed = (
        P(("dp", "seq"), None),
        P(("dp", "seq"), None),
        P(("dp", "seq"), None),
        P("seq", None),
        P(("dp", "seq"), None, None),
        P(("dp", "seq"), None),
    )
    return jax.shard_map(
        shards, mesh=mesh, in_specs=placed, out_specs=P(("dp", "seq"), None), check_vma=False
    )
```

```python
import functools

import jax
import jax.numpy as jnp
from jax import lax
from jax.experimental import pallas as pl
from jax.experimental.pallas import tpu as pltpu
from jax.sharding import PartitionSpec as P

HD = 128
BLOCK = 128
LEVELS = 3
DIRS = 2 * LEVELS
MASKED = -1e30
LEVEL_ORDER = (1, 2, 0)


def hop(direction):
    size = 2 ** (direction % LEVELS)
    return size if direction < LEVELS else -size


def kernel(
    n, q_ref, k_ref, v_ref, w_ref, picks_ref, counts_ref, out_ref, wout_ref,
    pack, mark, got, got_mark, acc, top, total,
    pack_send, pack_recv, mark_send, mark_recv, w_send, w_recv, own_sem,
):
    me = lax.axis_index("seq")
    dp = lax.axis_index("dp")
    sibling = dp + 1 - 2 * (dp % 2)
    rows, width = q_ref.shape
    heads = width // HD
    slots = picks_ref.shape[1]
    half_cols = w_ref.shape[1] // 2
    half = pl.ds(pl.multiple_of((dp % 2) * half_cols, half_cols), half_cols)

    near = me + 1 - 2 * (me % 2)
    others = n // 2

    def inside(shard):
        return jnp.logical_and(shard >= 0, shard < n)

    barrier = pltpu.get_barrier_semaphore()
    expected = jnp.int32(others + 1)
    for direction in range(DIRS):
        other = me + hop(direction)
        expected = expected + inside(other).astype(jnp.int32)

        @pl.when(inside(other))
        def _(other=other):
            pl.semaphore_signal(
                barrier, inc=1, device_id=(dp, other), device_id_type=pl.DeviceIdType.MESH
            )
    for other in [near] + [(me + 2 * j) % n for j in range(1, others)]:
        pl.semaphore_signal(
            barrier, inc=1, device_id=(dp, other), device_id_type=pl.DeviceIdType.MESH
        )
    pl.semaphore_signal(
        barrier, inc=1, device_id=(sibling, me), device_id_type=pl.DeviceIdType.MESH
    )

    own = pltpu.make_async_copy(w_ref.at[:, half], wout_ref.at[me, :, half], own_sem)
    own.start()

    def fill(direction, slot):
        block = picks_ref[direction, slot]
        pack[direction, slot, 0] = k_ref[block]
        pack[direction, slot, 1] = v_ref[block]

    def fill_mark(direction):
        for slot in range(slots):
            live = counts_ref[0, direction] > slot
            mark[direction, slot] = jnp.full((8, HD), jnp.where(live, 0.0, MASKED), jnp.float32)

    def pack_copy(direction, slot):
        return pltpu.make_async_remote_copy(
            pack.at[direction, slot],
            got.at[direction % LEVELS, slot, :, direction // LEVELS],
            pack_send.at[direction, slot], pack_recv.at[direction, slot],
            device_id=(dp, me + hop(direction)), device_id_type=pl.DeviceIdType.MESH,
        )

    def mark_copy(direction):
        return pltpu.make_async_remote_copy(
            mark.at[direction], got_mark.at[direction],
            mark_send.at[direction], mark_recv.at[direction],
            device_id=(dp, me + hop(direction)), device_id_type=pl.DeviceIdType.MESH,
        )

    def sibling_arrival(j, same):
        shard = ((me if same else near) + n - 2 * j) % n
        other_half = pl.ds(pl.multiple_of((1 - dp % 2) * half_cols, half_cols), half_cols)
        place = wout_ref.at[shard, :, other_half]
        index = n + j + (0 if same else others)
        return pltpu.make_async_remote_copy(
            place, place, w_send.at[index], w_recv.at[index],
            device_id=(sibling, me), device_id_type=pl.DeviceIdType.MESH,
        )

    def send(level, slot):
        for direction in (level, level + LEVELS):
            fill(direction, slot)
            if slot == 0:
                fill_mark(direction)

            @pl.when(inside(me + hop(direction)))
            def _(direction=direction):
                if slot == 0:
                    mark_copy(direction).start()
                pack_copy(direction, slot).start()

    def weight_copy(shard, index, to):
        place = wout_ref.at[shard, :, half]
        return pltpu.make_async_remote_copy(
            place, place, w_send.at[index], w_recv.at[index],
            device_id=to, device_id_type=pl.DeviceIdType.MESH,
        )

    def spread(j):
        return weight_copy(me, j, (dp, (me + 2 * j) % n))

    def spread_arrival(j):
        return weight_copy((me + n - 2 * j) % n, j, (dp, (me + 2 * j) % n))

    def across(j):
        return weight_copy((me + n - 2 * j) % n, others + j, (dp, near))

    def across_arrival(j):
        return weight_copy((near + n - 2 * j) % n, others + j, (dp, near))

    def pair(j, same):
        shard = ((me if same else near) + n - 2 * j) % n
        return weight_copy(shard, n + j + (0 if same else others), (sibling, me))

    for direction in range(DIRS):

        @pl.when(jnp.logical_not(inside(me - hop(direction))))
        def _(direction=direction):
            for slot in range(slots):
                for kind in range(2):
                    got[direction % LEVELS, slot, kind, direction // LEVELS] = jnp.zeros(
                        (BLOCK, width), jnp.bfloat16
                    )
            got_mark[direction] = jnp.full((slots, 8, HD), MASKED, jnp.float32)

    pl.semaphore_wait(barrier, expected)
    own.wait()
    for j in range(1, others):
        spread(j).start()
    across(0).start()
    pair(0, True).start()
    for level in LEVEL_ORDER[:2]:
        send(level, 0)

    scale = HD**-0.5
    tiles = 2
    tile = rows // tiles

    def local_head(h, carry):
        cols = pl.ds(pl.multiple_of(h * HD, HD), HD)
        keys = k_ref[:, :, cols].reshape(rows, HD)
        values = v_ref[:, :, cols].reshape(rows, HD)
        for t in range(tiles):
            at = pl.ds(t * tile, tile)
            scores = lax.dot_general(
                q_ref[at, cols], keys, (((1,), (1,)), ((), ())),
                preferred_element_type=jnp.float32,
            ) * scale
            high = jnp.max(scores, axis=1, keepdims=True)
            weights = jnp.exp(scores - high)
            top[h, at, :] = high
            total[h, at, :] = jnp.sum(weights, axis=1, keepdims=True)
            acc[h, at, :] = jnp.dot(
                weights.astype(jnp.bfloat16), values, preferred_element_type=jnp.float32
            )
        return carry

    lax.fori_loop(0, heads // 2, local_head, 0)
    for j in range(1, others):
        spread_arrival(j).wait_recv()
        across(j).start()
        pair(j, True).start()
    for level in LEVEL_ORDER[2:]:
        send(level, 0)
    lax.fori_loop(heads // 2, heads, local_head, 0)
    send(LEVEL_ORDER[0], 1)

    def far_head(level, slot, h):
        cols = pl.ds(pl.multiple_of(h * HD, HD), HD)
        keys = got[level, slot, 0, :, :, cols].reshape(2 * BLOCK, HD)
        values = got[level, slot, 1, :, :, cols].reshape(2 * BLOCK, HD)
        bias = jnp.concatenate(
            [got_mark[direction, slot, 0:1, :] for direction in (level, level + LEVELS)], axis=1
        )
        for t in range(tiles):
            at = pl.ds(t * tile, tile)
            scores = lax.dot_general(
                q_ref[at, cols], keys, (((1,), (1,)), ((), ())),
                preferred_element_type=jnp.float32,
            ) * scale + bias
            before = top[h, at, :]
            high = jnp.maximum(before, jnp.max(scores, axis=1, keepdims=True))
            shrink = jnp.exp(before - high)
            weights = jnp.exp(scores - high)
            top[h, at, :] = high
            total[h, at, :] = total[h, at, :] * shrink + jnp.sum(weights, axis=1, keepdims=True)
            acc[h, at, :] = acc[h, at, :] * shrink + jnp.dot(
                weights.astype(jnp.bfloat16), values, preferred_element_type=jnp.float32
            )

    def far(level, slot):
        for direction in (level, level + LEVELS):

            @pl.when(inside(me - hop(direction)))
            def _(direction=direction):
                if slot == 0:
                    mark_copy(direction).wait_recv()
                pack_copy(direction, slot).wait_recv()

        def body(h, carry):
            far_head(level, slot, h)
            return carry

        lax.fori_loop(0, heads, body, 0, unroll=3)

    far(LEVEL_ORDER[0], 0)
    for j in range(others):
        across_arrival(j).wait_recv()
        pair(j, False).start()
    for level in LEVEL_ORDER[1:]:
        send(level, 1)
    for level in LEVEL_ORDER[1:]:
        far(level, 0)
    for slot in range(1, slots):
        for level in LEVEL_ORDER:
            far(level, slot)

    for h in range(heads):
        out_ref[:, h * HD : (h + 1) * HD] = (acc[h] / total[h]).astype(out_ref.dtype)

    for direction in range(DIRS):

        @pl.when(inside(me + hop(direction)))
        def _(direction=direction):
            mark_copy(direction).wait_send()
            for slot in range(slots):
                pack_copy(direction, slot).wait_send()

    for j in range(others):
        if j > 0:
            spread(j).wait_send()
        across(j).wait_send()
    for same in (True, False):
        for j in range(others):
            pair(j, same).wait_send()
            sibling_arrival(j, same).wait_recv()


def shards(queries, key_states, value_states, out_weight, block_picks, slot_counts):
    n = lax.axis_size("seq")
    rows, width = queries.shape
    slots = block_picks.shape[2]
    heads = width // HD
    blocks = rows // BLOCK
    vmem = pl.BlockSpec(memory_space=pltpu.VMEM)
    smem = pl.BlockSpec(memory_space=pltpu.SMEM)
    dma = pltpu.SemaphoreType.DMA
    attended, weight = pl.pallas_call(
        functools.partial(kernel, n),
        out_shape=(
            jax.ShapeDtypeStruct((rows, width), jnp.bfloat16),
            jax.ShapeDtypeStruct((n,) + out_weight.shape, jnp.bfloat16),
        ),
        in_specs=[vmem, vmem, vmem, vmem, smem, smem],
        out_specs=(vmem, pl.BlockSpec(memory_space=pl.ANY)),
        scratch_shapes=[
            pltpu.VMEM((DIRS, slots, 2, BLOCK, width), jnp.bfloat16),
            pltpu.VMEM((DIRS, slots, 8, HD), jnp.float32),
            pltpu.VMEM((LEVELS, slots, 2, 2, BLOCK, width), jnp.bfloat16),
            pltpu.VMEM((DIRS, slots, 8, HD), jnp.float32),
            pltpu.VMEM((heads, rows, HD), jnp.float32),
            pltpu.VMEM((heads, rows, 1), jnp.float32),
            pltpu.VMEM((heads, rows, 1), jnp.float32),
            dma((DIRS, slots)), dma((DIRS, slots)), dma((DIRS,)), dma((DIRS,)),
            dma((2 * n,)), dma((2 * n,)), dma,
        ],
        compiler_params=pltpu.CompilerParams(
            collective_id=0, has_side_effects=True, vmem_limit_bytes=48 * 2**20
        ),
    )(
        queries,
        key_states.reshape(blocks, BLOCK, width),
        value_states.reshape(blocks, BLOCK, width),
        out_weight,
        block_picks[0],
        slot_counts,
    )
    result = jnp.dot(
        attended, weight.reshape(-1, weight.shape[2]), preferred_element_type=jnp.float32
    )
    return result.astype(jnp.bfloat16)


def solution(mesh):
    placed = (
        P(("dp", "seq"), None),
        P(("dp", "seq"), None),
        P(("dp", "seq"), None),
        P("seq", None),
        P(("dp", "seq"), None, None),
        P(("dp", "seq"), None),
    )
    return jax.shard_map(
        shards, mesh=mesh, in_specs=placed, out_specs=P(("dp", "seq"), None), check_vma=False
    )
```
